32 devices in a mesh: groups: 2 (over y), col: 16 (over z, x, core).
Axes of the slice: x: 2, y: 2, z: 4, core: 2. Of those that a mesh axis runs over, the one named last changes fastest.
Arguments:
- cooccur_slab: bfloat16 [4096, 32768], P('groups', 'col'), parts along dimension 0, may hold values from 0 to 0.4861359, as said below
- test_matrix: bfloat16 [32768, 256], P('col'), may hold values from -0.03125 to 0.03125
Outputs:
- projection: float32 [512, 32768], P('groups', 'col'), parts along dimension 0
The draws below stay inside these ranges and needn't reach their ends.
There are 2 independent parts, one for each index of `groups`. The reference program is written for one: setup_inputs(seed, part) draws one part's arguments, and reference() takes and returns one part's arrays. A program takes and returns all parts, laid end to end along the dimension named above; an argument that names none is the same for every part. Nothing has to cross between parts.
Inputs may be any that keep to these rules, and one draw needn't show every extreme that they name: `cooccur_slab`: entries are non-negative, as in a positive PMI matrix.
All inputs are finite; a program needn't handle non-finite values.
Results may differ from the reference program's by a relative error of at most 0.0018.
Values may be sent and summed in bfloat16 or wider, within the bound.
A program may use at most 64 MiB of HBM per device.

```python
import math
import jax
import jax.numpy as jnp
from jax import lax

ROWS = 2048
K = 256
COLS = 32768


def draw_cooccur_slab(key, part):
    key = jax.random.fold_in(key, 11)
    noise_key, row_key, col_key = jax.random.split(key, 3)
    noise = jnp.clip(jax.random.normal(noise_key, (ROWS, COLS), jnp.float32), -4.0, 4.0)
    position = jnp.arange(ROWS, dtype=jnp.float32).reshape(ROWS, 1) / ROWS
    row_scale = jnp.exp(jax.random.uniform(row_key, (ROWS, 1), jnp.float32, 0.0, math.log(10.0 / 3.0))) * (1.0 + 2.0 * position)
    col_scale = jnp.exp(jax.random.uniform(col_key, (1, COLS), jnp.float32, 0.0, math.log(10.0)))
    values = jnp.maximum(noise + 0.3, 0.0) * row_scale * col_scale * (0.05 / math.sqrt(ROWS))
    return values.astype(jnp.bfloat16)


def block_scale(key, shape, cuts, least, largest):
    level, own = 1.0, jax.random.fold_in(key, 6)
    for dim, blocks in cuts:
        heights = jnp.exp(jax.random.uniform(jax.random.fold_in(own, dim), (blocks,), jnp.float32, least / len(cuts), largest / len(cuts)))
        level = level * jnp.repeat(heights, shape[dim] // blocks).reshape([-1 if axis == dim else 1 for axis in range(len(shape))])
    return level


def gaussian(rng, dims, scale, bound, cuts=(), kind=jnp.bfloat16):
    array = scale * jax.random.normal(rng, dims, jnp.float32)
    if cuts:
        array = array * block_scale(rng, dims, cuts, -0.22, 0.18)
    return jnp.clip(array, -bound, bound).astype(kind)


def setup_inputs(seed: int = 0, part: int = 0) -> dict:
    key_list = jax.random.split(jax.random.key(seed), 3)
    part_keys = jax.random.split(jax.random.fold_in(key_list[2], part), 3)
    return {
        "cooccur_slab": draw_cooccur_slab(jax.random.fold_in(jax.random.fold_in(key_list[2], part), 71), part),
        "test_matrix": gaussian(key_list[1], (COLS, K), COLS ** -0.5, 0.03125, ((0, 16),)),
    }


def reference(cooccur_slab, test_matrix):
    sketch = jnp.dot(cooccur_slab.astype(jnp.float32), test_matrix.astype(jnp.float32), preferred_element_type=jnp.float32)
    gram_matrix = jnp.dot(sketch.T, sketch, precision=lax.Precision.HIGHEST)
    lower_factor = jnp.linalg.cholesky(gram_matrix)
    orthobasis = jax.scipy.linalg.solve_triangular(lower_factor, sketch.T, lower=True).T.astype(jnp.bfloat16)
    return jnp.dot(orthobasis.T.astype(jnp.float32), cooccur_slab.astype(jnp.float32), preferred_element_type=jnp.float32)
```

```python
import functools

import jax
import jax.numpy as jnp
from jax import lax
from jax.experimental import pallas as pl
from jax.experimental.pallas import tpu as pltpu
from jax.sharding import PartitionSpec as P

F32 = jnp.float32
BF16 = jnp.bfloat16
MESH = pl.DeviceIdType.MESH
HIGHEST = lax.Precision.HIGHEST


def sketch_kernel(
    nx, nz, nch, slab_hbm, test_hbm, gram_ref, cross_ref,
    slab, test, part, core_in, half, x_in, quarter, z_in, sketch, split,
    load_sem, core_sem, x_sem, z_sem, gz_sem, gx_sem, gc_sem,
):
    ncol = 2 * nx * nz
    rows, width = slab.shape
    k = test.shape[1]
    rc = rows // nch
    hr, xr, own = rc // 2, rc // (2 * nx), rc // ncol
    me = lax.axis_index("col")
    c = lax.rem(me, 2)
    x = lax.rem(me // 2, nx)
    z = me // (2 * nx)

    def device(z_, x_, c_):
        return {"col": (z_ * nx + x_) * 2 + c_}

    core_peer = device(z, x, 1 - c)
    x_peers = [lax.rem(x + d, nx) for d in range(1, nx)]
    z_peers = [lax.rem(z + d, nz) for d in range(1, nz)]

    load_test = pltpu.make_async_copy(test_hbm, test, load_sem.at[nch])
    load_test.start()
    loads = []
    for q in range(nch):
        at = pl.ds(q * rc, rc)
        load = pltpu.make_async_copy(slab_hbm.at[at], slab.at[at], load_sem.at[q])
        load.start()
        loads.append(load)

    barrier = pltpu.get_barrier_semaphore()
    peers = [core_peer] + [device(z, p, c) for p in x_peers] + [device(p, x, c) for p in z_peers]
    for peer in peers:
        pl.semaphore_signal(barrier, inc=1, device_id=peer, device_id_type=MESH)

    def remote(src, dst, sems, index, peer):
        return pltpu.make_async_remote_copy(
            src_ref=src, dst_ref=dst,
            send_sem=sems.at[(0,) + index], recv_sem=sems.at[(1,) + index],
            device_id=peer, device_id_type=MESH,
        )

    sent = []
    flights = {}

    def start(name, q, copies):
        for copy in copies:
            copy.start()
        sent.extend(copies)
        flights[name, q] = copies

    def arrive(name, q):
        for copy in flights[name, q]:
            copy.wait_recv()

    def rows_at(first, size):
        return pl.ds(pl.multiple_of(first, 8), size)

    def stage_compute(q):
        if q == 0:
            load_test.wait()
        loads[q].wait()
        tile = 128

        @pl.loop(0, rc // tile)
        def _(i):
            at = rows_at(q * rc + i * tile, tile)
            part[at, :] = jnp.dot(slab[at, :], test[...], preferred_element_type=F32)

        if q == 0:
            pl.semaphore_wait(barrier, len(peers))
        src = part.at[rows_at(q * rc + (1 - c) * hr, hr)]
        start("core", q, [remote(src, core_in.at[q], core_sem, (q,), core_peer)])

    def stage_core(q):
        arrive("core", q)
        half[q] = part[rows_at(q * rc + c * hr, hr), :] + core_in[q]
        start("x", q, [
            remote(half.at[q, rows_at(p * xr, xr)], x_in.at[q, d], x_sem, (q, d), device(z, p, c))
            for d, p in enumerate(x_peers)
        ])

    def stage_x(q):
        arrive("x", q)
        total = half[q, rows_at(x * xr, xr), :]
        for d in range(nx - 1):
            total = total + x_in[q, d]
        quarter[q] = total
        start("z", q, [
            remote(quarter.at[q, rows_at(p * own, own)], z_in.at[q, d], z_sem, (q, d), device(p, x, c))
            for d, p in enumerate(z_peers)
        ])

    def stage_z(q):
        arrive("z", q)
        total = quarter[q, rows_at(z * own, own), :]
        for d in range(nz - 1):
            total = total + z_in[q, d]
        at = rows_at(q * rc + c * hr + x * xr + z * own, own)
        sketch[at, :] = total
        start("gz", q, [
            remote(sketch.at[at], sketch.at[at], gz_sem, (q, d), device(p, x, c))
            for d, p in enumerate(z_peers)
        ])

    def stage_gz(q):
        arrive("gz", q)
        at = rows_at(q * rc + c * hr + x * xr, xr)
        start("gx", q, [
            remote(sketch.at[at], sketch.at[at], gx_sem, (q, d), device(z, p, c))
            for d, p in enumerate(x_peers)
        ])

    def stage_gx(q):
        arrive("gx", q)
        at = rows_at(q * rc + c * hr, hr)
        start("gc", q, [remote(sketch.at[at], sketch.at[at], gc_sem, (q,), core_peer)])

    def stage_gc(q):
        arrive("gc", q)
        at = pl.ds(q * rc, rc)
        block = sketch[at, :]
        turned = block.T
        gram = jnp.dot(turned, block, precision=HIGHEST, preferred_element_type=F32)
        gram_ref[...] = gram if q == 0 else gram_ref[...] + gram
        high = turned.astype(BF16)
        split[0:k, :] = high
        split[k:2 * k, :] = (turned - high.astype(F32)).astype(BF16)
        tile = 256

        @pl.loop(0, width // tile)
        def _(i):
            cols = pl.ds(pl.multiple_of(i * tile, tile), tile)
            both = jnp.dot(split[...], slab[at, cols], preferred_element_type=F32)
            cross = both[0:k] + both[k:2 * k]
            cross_ref[:, cols] = cross if q == 0 else cross_ref[:, cols] + cross

    stages = [stage_compute, stage_core, stage_x, stage_z, stage_gz, stage_gx, stage_gc]
    for t in range(nch + len(stages) - 1):
        for s in reversed(range(len(stages))):
            if 0 <= t - s < nch:
                stages[s](t - s)
    for copy in sent:
        copy.wait_send()


def factor_kernel(gram_ref, cross_ref, out_ref, work, inverse):
    k = gram_ref.shape[0]
    block, panel, lanes = 32, 8, 128
    work[:, 0:k] = gram_ref[...]
    row_at = lax.broadcasted_iota(jnp.int32, (k, k), 0)
    col_at = lax.broadcasted_iota(jnp.int32, (k, k), 1)
    work[:, k:2 * k] = (row_at == col_at).astype(F32)
    sub = lax.broadcasted_iota(jnp.int32, (block, lanes), 0)
    for b in range(k // block):
        first = b * block
        strips = [work[first:first + block, j * lanes:(j + 1) * lanes] for j in range(2 * k // lanes)]
        scale = jnp.zeros((block, lanes), F32)
        for p in range(block // panel):
            base = first + p * panel
            strip, lane = base // lanes, base % lanes
            columns = [
                jnp.broadcast_to(strips[strip][:, lane + i:lane + i + 1], (block, lanes)) for i in range(panel)
            ]
            for i in range(panel):
                r = p * panel + i
                pivot = columns[i][r:r + 1, :]
                scale = jnp.where(sub == r, lax.rsqrt(pivot), scale)
                if r + 1 == block:
                    continue
                lower = jnp.where(sub > r, columns[i] * (1.0 / pivot), 0.0)
                for j in range(i + 1, panel):
                    columns[j] = columns[j] - lower * columns[j][r:r + 1, :]
                strips = [s - lower * s[r:r + 1, :] for s in strips]
        done = jnp.concatenate([s * scale for s in strips], axis=1)
        inverse[first:first + block, :] = done[:, k:2 * k]
        if first + block < k:
            after = first + block
            update = lax.dot_general(
                done[:, after:k], done, (((0,), (0,)), ((), ())),
                precision=HIGHEST, preferred_element_type=F32,
            )
            work[after:k, :] = work[after:k, :] - update

    tile = 256

    @pl.loop(0, cross_ref.shape[1] // tile)
    def _(i):
        cols = pl.ds(pl.multiple_of(i * tile, tile), tile)
        out_ref[:, cols] = jnp.dot(
            inverse[...], cross_ref[:, cols], precision=HIGHEST, preferred_element_type=F32
        )


def local(ncol, slab, test):
    rows, width = slab.shape
    k = test.shape[1]
    chips = ncol // 2
    nx = 2 ** (chips.bit_length() // 3) if chips > 1 else 1
    nz = chips // nx
    nch = max(1, min(4, rows // (8 * ncol)))
    rc = rows // nch
    hr, xr, own = rc // 2, rc // (2 * nx), rc // ncol
    dma = pltpu.SemaphoreType.DMA
    gram, cross = pl.pallas_call(
        functools.partial(sketch_kernel, nx, nz, nch),
        out_shape=(jax.ShapeDtypeStruct((k, k), F32), jax.ShapeDtypeStruct((k, width), F32)),
        in_specs=[pl.BlockSpec(memory_space=pl.ANY)] * 2,
        out_specs=(pl.BlockSpec(memory_space=pltpu.VMEM),) * 2,
        scratch_shapes=[
            pltpu.VMEM((rows, width), BF16),
            pltpu.VMEM((width, k), BF16),
            pltpu.VMEM((rows, k), F32),
            pltpu.VMEM((nch, hr, k), F32),
            pltpu.VMEM((nch, hr, k), F32),
            pltpu.VMEM((nch, nx - 1, xr, k), F32),
            pltpu.VMEM((nch, xr, k), F32),
            pltpu.VMEM((nch, nz - 1, own, k), F32),
            pltpu.VMEM((rows, k), F32),
            pltpu.VMEM((2 * k, rc), BF16),
            dma((nch + 1,)),
            dma((2, nch)),
            dma((2, nch, nx - 1)),
            dma((2, nch, nz - 1)),
            dma((2, nch, nz - 1)),
            dma((2, nch, nx - 1)),
            dma((2, nch)),
        ],
        compiler_params=pltpu.CompilerParams(
            collective_id=0, has_side_effects=True, vmem_limit_bytes=48 * 2 ** 20
        ),
    )(slab, test)
    return pl.pallas_call(
        factor_kernel,
        out_shape=jax.ShapeDtypeStruct((k, width), F32),
        in_specs=[pl.BlockSpec(memory_space=pltpu.VMEM)] * 2,
        out_specs=pl.BlockSpec(memory_space=pltpu.VMEM),
        scratch_shapes=[pltpu.VMEM((k, 2 * k), F32), pltpu.VMEM((k, k), F32)],
        compiler_params=pltpu.CompilerParams(vmem_limit_bytes=32 * 2 ** 20),
    )(gram, cross)


def solution(mesh):
    return jax.shard_map(
        functools.partial(local, mesh.shape["col"]),
        mesh=mesh,
        in_specs=(P("groups", "col"), P("col", None)),
        out_specs=P("groups", "col"),
        check_vma=False,
    )
```

```python
import functools

import jax
import jax.numpy as jnp
from jax import lax
from jax.experimental import pallas as pl
from jax.experimental.pallas import tpu as pltpu
from jax.sharding import PartitionSpec as P

F32 = jnp.float32
BF16 = jnp.bfloat16
MESH = pl.DeviceIdType.MESH
HIGHEST = lax.Precision.HIGHEST


def factor(gram_ref, inverse, work, steps):
    k = gram_ref.shape[0]
    block, panel, lanes = 32, 8, 128
    work[:, 0:k] = gram_ref[...]
    row_at = lax.broadcasted_iota(jnp.int32, (k, k), 0)
    col_at = lax.broadcasted_iota(jnp.int32, (k, k), 1)
    work[:, k:2 * k] = (row_at == col_at).astype(F32)
    sub = lax.broadcasted_iota(jnp.int32, (block, lanes), 0)
    plan = {1: 1, 3: 2, 4: 1, 5: 2, 6: 1, 7: 1}
    for b in range(k // block):
        for _ in range(plan.get(b, 0)):
            if steps:
                steps.pop(0)()
        first = b * block
        strips = [work[first:first + block, j * lanes:(j + 1) * lanes] for j in range(2 * k // lanes)]
        scale = jnp.zeros((block, lanes), F32)
        for p in range(block // panel):
            base = first + p * panel
            strip, lane = base // lanes, base % lanes
            columns = [
                jnp.broadcast_to(strips[strip][:, lane + i:lane + i + 1], (block, lanes)) for i in range(panel)
            ]
            for i in range(panel):
                r = p * panel + i
                pivot = columns[i][r:r + 1, :]
                scale = jnp.where(sub == r, lax.rsqrt(pivot), scale)
                if r + 1 == block:
                    continue
                lower = jnp.where(sub > r, columns[i] * (1.0 / pivot), 0.0)
                for j in range(i + 1, panel):
                    columns[j] = columns[j] - lower * columns[j][r:r + 1, :]
                strips = [s - lower * s[r:r + 1, :] for s in strips]
        done = jnp.concatenate([s * scale for s in strips], axis=1)
        inverse[first:first + block, :] = done[:, k:2 * k]
        if first + block < k:
            after = first + block
            update = lax.dot_general(
                done[:, after:k], done, (((0,), (0,)), ((), ())),
                precision=HIGHEST, preferred_element_type=F32,
            )
            work[after:k, :] = work[after:k, :] - update
    return steps


def project_kernel(inverse_ref, cross_ref, out_ref):
    out_ref[...] = jnp.dot(
        inverse_ref[...], cross_ref[...], precision=HIGHEST, preferred_element_type=F32
    )


def sketch_kernel(
    nx, nz, nch, slab_hbm, test_hbm, inverse_ref, cross_ref,
    slab, test, part, core_in, half, x_in, quarter, z_in, sketch, split,
    gram_own, gram_c_in, gram_c, gram_x_in, gram_x, gram_z_in, gram, work,
    load_sem, core_sem, x_sem, z_sem, gz_sem, gx_sem, gc_sem,
    rc_sem, rx_sem, rz_sem, bz_sem, bx_sem, bc_sem,
):
    ncol = 2 * nx * nz
    rows, width = slab.shape
    k = test.shape[1]
    rc = rows // nch
    hr, xr, own = rc // 2, rc // (2 * nx), rc // ncol
    me = lax.axis_index("col")
    c = lax.rem(me, 2)
    x = lax.rem(me // 2, nx)
    z = me // (2 * nx)

    def device(z_, x_, c_):
        return {"col": (z_ * nx + x_) * 2 + c_}

    core_peer = device(z, x, 1 - c)
    x_peers = [lax.rem(x + d, nx) for d in range(1, nx)]
    z_peers = [lax.rem(z + d, nz) for d in range(1, nz)]

    load_test = pltpu.make_async_copy(test_hbm, test, load_sem.at[nch])
    load_test.start()
    loads = []
    for q in range(nch):
        at = pl.ds(q * rc, rc)
        load = pltpu.make_async_copy(slab_hbm.at[at], slab.at[at], load_sem.at[q])
        load.start()
        loads.append(load)

    barrier = pltpu.get_barrier_semaphore()
    peers = [core_peer] + [device(z, p, c) for p in x_peers] + [device(p, x, c) for p in z_peers]
    for peer in peers:
        pl.semaphore_signal(barrier, inc=1, device_id=peer, device_id_type=MESH)

    def remote(src, dst, sems, index, peer):
        return pltpu.make_async_remote_copy(
            src_ref=src, dst_ref=dst,
            send_sem=sems.at[(0,) + index], recv_sem=sems.at[(1,) + index],
            device_id=peer, device_id_type=MESH,
        )

    sent = []
    flights = {}

    def start(name, q, copies):
        for copy in copies:
            copy.start()
        sent.extend(copies)
        flights[name, q] = copies

    def arrive(name, q):
        for copy in flights[name, q]:
            copy.wait_recv()

    def rows_at(first, size):
        return pl.ds(pl.multiple_of(first, 8), size)

    def stage_compute(q):
        if q == 0:
            load_test.wait()
        loads[q].wait()
        tile = 256

        @pl.loop(0, rc // tile)
        def _(i):
            at = rows_at(q * rc + i * tile, tile)
            part[at, :] = jnp.dot(slab[at, :], test[...], preferred_element_type=F32)

        if q == 0:
            pl.semaphore_wait(barrier, len(peers))
        src = part.at[rows_at(q * rc + (1 - c) * hr, hr)]
        start("core", q, [remote(src, core_in.at[q], core_sem, (q,), core_peer)])

    def stage_core(q):
        arrive("core", q)
        half[q] = part[rows_at(q * rc + c * hr, hr), :] + core_in[q]
        start("x", q, [
            remote(half.at[q, rows_at(p * xr, xr)], x_in.at[q, d], x_sem, (q, d), device(z, p, c))
            for d, p in enumerate(x_peers)
        ])

    def stage_x(q):
        arrive("x", q)
        total = half[q, rows_at(x * xr, xr), :]
        for d in range(nx - 1):
            total = total + x_in[q, d]
        quarter[q] = total
        start("z", q, [
            remote(quarter.at[q, rows_at(p * own, own)], z_in.at[q, d], z_sem, (q, d), device(p, x, c))
            for d, p in enumerate(z_peers)
        ])

    def stage_z(q):
        arrive("z", q)
        total = quarter[q, rows_at(z * own, own), :]
        for d in range(nz - 1):
            total = total + z_in[q, d]
        at = rows_at(q * rc + c * hr + x * xr + z * own, own)
        sketch[at, :] = total
        square = lax.dot_general(
            total, total, (((0,), (0,)), ((), ())), precision=HIGHEST, preferred_element_type=F32
        )
        gram_own[...] = square if q == 0 else gram_own[...] + square

    def gather_z(q):
        at = rows_at(q * rc + c * hr + x * xr + z * own, own)
        start("gz", q, [
            remote(sketch.at[at], sketch.at[at], gz_sem, (q, d), device(p, x, c))
            for d, p in enumerate(z_peers)
        ])

    def gather_x(q):
        arrive("gz", q)
        at = rows_at(q * rc + c * hr + x * xr, xr)
        start("gx", q, [
            remote(sketch.at[at], sketch.at[at], gx_sem, (q, d), device(z, p, c))
            for d, p in enumerate(x_peers)
        ])

    def gather_core(q):
        arrive("gx", q)
        at = rows_at(q * rc + c * hr, hr)
        start("gc", q, [remote(sketch.at[at], sketch.at[at], gc_sem, (q,), core_peer)])

    def cross(q):
        arrive("gc", q)
        at = pl.ds(q * rc, rc)
        block = sketch[at, :]
        turned = block.T
        high = turned.astype(BF16)
        split[0:k, :] = high
        split[k:2 * k, :] = (turned - high.astype(F32)).astype(BF16)
        tile = 256

        @pl.loop(0, width // tile)
        def _(i):
            cols = pl.ds(pl.multiple_of(i * tile, tile), tile)
            both = jnp.dot(split[...], slab[at, cols], preferred_element_type=F32)
            term = both[0:k] + both[k:2 * k]
            cross_ref[:, cols] = term if q == 0 else cross_ref[:, cols] + term

    stages = [stage_compute, stage_core, stage_x, stage_z]
    for t in range(nch + len(stages) - 1):
        for s in reversed(range(len(stages))):
            if 0 <= t - s < nch:
                stages[s](t - s)

    kc, kx, kz = k // 2, k // (2 * nx), k // ncol
    start("rc", 0, [remote(gram_own.at[rows_at((1 - c) * kc, kc)], gram_c_in, rc_sem, (0,), core_peer)])
    arrive("rc", 0)
    gram_c[...] = gram_own[rows_at(c * kc, kc), :] + gram_c_in[...]
    start("rx", 0, [
        remote(gram_c.at[rows_at(p * kx, kx)], gram_x_in.at[d], rx_sem, (d,), device(z, p, c))
        for d, p in enumerate(x_peers)
    ])
    arrive("rx", 0)
    total = gram_c[rows_at(x * kx, kx), :]
    for d in range(nx - 1):
        total = total + gram_x_in[d]
    gram_x[...] = total
    spread = kz >= 8
    start("rz", 0, [
        remote(gram_x.at[rows_at(p * kz, kz)] if spread else gram_x, gram_z_in.at[d], rz_sem, (d,), device(p, x, c))
        for d, p in enumerate(z_peers)
    ])
    arrive("rz", 0)
    total = gram_x[rows_at(z * kz, kz), :] if spread else total
    for d in range(nz - 1):
        total = total + gram_z_in[d]
    if spread:
        at = rows_at(c * kc + x * kx + z * kz, kz)
        gram[at, :] = total
        start("bz", 0, [
            remote(gram.at[at], gram.at[at], bz_sem, (d,), device(p, x, c)) for d, p in enumerate(z_peers)
        ])
        gather_z(0)
        arrive("bz", 0)
    else:
        gram[rows_at(c * kc + x * kx, kx), :] = total
        gather_z(0)
    at = rows_at(c * kc + x * kx, kx)
    start("bx", 0, [
        remote(gram.at[at], gram.at[at], bx_sem, (d,), device(z, p, c)) for d, p in enumerate(x_peers)
    ])
    for q in range(1, nch):
        gather_z(q)
    arrive("bx", 0)
    at = rows_at(c * kc, kc)
    start("bc", 0, [remote(gram.at[at], gram.at[at], bc_sem, (0,), core_peer)])
    arrive("bc", 0)

    steps = []
    for t in range(nch + 2):
        if t < nch:
            steps.append(functools.partial(gather_x, t))
        if 1 <= t <= nch:
            steps.append(functools.partial(gather_core, t - 1))
        if t >= 2:
            steps.append(functools.partial(cross, t - 2))
    left = factor(gram, inverse_ref, work, steps)
    for step in left:
        step()
    for copy in sent:
        copy.wait_send()


def local(ncol, slab, test):
    rows, width = slab.shape
    k = test.shape[1]
    chips = ncol // 2
    nx = 2 ** (chips.bit_length() // 3) if chips > 1 else 1
    nz = chips // nx
    nch = max(1, min(4, rows // (8 * ncol)))
    rc = rows // nch
    hr, xr, own = rc // 2, rc // (2 * nx), rc // ncol
    dma = pltpu.SemaphoreType.DMA
    kc, kx, kz = k // 2, k // (2 * nx), k // ncol
    inverse, cross = pl.pallas_call(
        functools.partial(sketch_kernel, nx, nz, nch),
        out_shape=(jax.ShapeDtypeStruct((k, k), F32), jax.ShapeDtypeStruct((k, width), F32)),
        in_specs=[pl.BlockSpec(memory_space=pltpu.HBM)] * 2,
        out_specs=(pl.BlockSpec(memory_space=pltpu.VMEM),) * 2,
        scratch_shapes=[
            pltpu.VMEM((rows, width), BF16),
            pltpu.VMEM((width, k), BF16),
            pltpu.VMEM((rows, k), F32),
            pltpu.VMEM((nch, hr, k), F32),
            pltpu.VMEM((nch, hr, k), F32),
            pltpu.VMEM((nch, nx - 1, xr, k), F32),
            pltpu.VMEM((nch, xr, k), F32),
            pltpu.VMEM((nch, nz - 1, own, k), F32),
            pltpu.VMEM((rows, k), F32),
            pltpu.VMEM((2 * k, rc), BF16),
            pltpu.VMEM((k, k), F32),
            pltpu.VMEM((kc, k), F32),
            pltpu.VMEM((kc, k), F32),
            pltpu.VMEM((nx - 1, kx, k), F32),
            pltpu.VMEM((kx, k), F32),
            pltpu.VMEM((nz - 1, kz if kz >= 8 else kx, k), F32),
            pltpu.VMEM((k, k), F32),
            pltpu.VMEM((k, 2 * k), F32),
            dma((nch + 1,)),
            dma((2, nch)),
            dma((2, nch, nx - 1)),
            dma((2, nch, nz - 1)),
            dma((2, nch, nz - 1)),
            dma((2, nch, nx - 1)),
            dma((2, nch)),
            dma((2, 1)),
            dma((2, nx - 1)),
            dma((2, nz - 1)),
            dma((2, nz - 1)),
            dma((2, nx - 1)),
            dma((2, 1)),
        ],
        compiler_params=pltpu.CompilerParams(
            collective_id=0, has_side_effects=True, vmem_limit_bytes=48 * 2 ** 20
        ),
    )(slab, test)
    tile = 512
    return pl.pallas_call(
        project_kernel,
        grid=(width // tile,),
        out_shape=jax.ShapeDtypeStruct((k, width), F32),
        in_specs=[
            pl.BlockSpec((k, k), lambda i: (0, 0)),
            pl.BlockSpec((k, tile), lambda i: (0, i)),
        ],
        out_specs=pl.BlockSpec((k, tile), lambda i: (0, i)),
        compiler_params=pltpu.CompilerParams(vmem_limit_bytes=24 * 2 ** 20),
    )(inverse, cross)


def solution(mesh):
    return jax.shard_map(
        functools.partial(local, mesh.shape["col"]),
        mesh=mesh,
        in_specs=(P("groups", "col"), P("col", None)),
        out_specs=P("groups", "col"),
        check_vma=False,
    )
```

```python
import functools

import jax
import jax.numpy as jnp
from jax import lax
from jax.experimental import pallas as pl
from jax.experimental.pallas import tpu as pltpu
from jax.sharding import PartitionSpec as P

F32 = jnp.float32
BF16 = jnp.bfloat16
MESH = pl.DeviceIdType.MESH
HIGHEST = lax.Precision.HIGHEST


def sketch_kernel(
    nx, nz, nch, slab_hbm, test_hbm, gram_ref, cross_ref,
    slab, test, part, core_in, half, x_in, quarter, z_in, sketch, split,
    load_sem, core_sem, x_sem, z_sem, gz_sem, gx_sem, gc_sem,
):
    ncol = 2 * nx * nz
    rows, width = slab.shape
    k = test.shape[1]
    rc = rows // nch
    hr, xr, own = rc // 2, rc // (2 * nx), rc // ncol
    me = lax.axis_index("col")
    c = lax.rem(me, 2)
    x = lax.rem(me // 2, nx)
    z = me // (2 * nx)

    def device(z_, x_, c_):
        return {"col": (z_ * nx + x_) * 2 + c_}

    core_peer = device(z, x, 1 - c)
    x_peers = [lax.rem(x + d, nx) for d in range(1, nx)]
    z_peers = [lax.rem(z + d, nz) for d in range(1, nz)]

    load_test = pltpu.make_async_copy(test_hbm, test, load_sem.at[nch])
    load_test.start()
    loads = []
    for q in range(nch):
        at = pl.ds(q * rc, rc)
        load = pltpu.make_async_copy(slab_hbm.at[at], slab.at[at], load_sem.at[q])
        load.start()
        loads.append(load)

    barrier = pltpu.get_barrier_semaphore()
    peers = [core_peer] + [device(z, p, c) for p in x_peers] + [device(p, x, c) for p in z_peers]
    for peer in peers:
        pl.semaphore_signal(barrier, inc=1, device_id=peer, device_id_type=MESH)

    def remote(src, dst, sems, index, peer):
        return pltpu.make_async_remote_copy(
            src_ref=src, dst_ref=dst,
            send_sem=sems.at[(0,) + index], recv_sem=sems.at[(1,) + index],
            device_id=peer, device_id_type=MESH,
        )

    sent = []
    flights = {}

    def start(name, q, copies):
        for copy in copies:
            copy.start()
        sent.extend(copies)
        flights[name, q] = copies

    def arrive(name, q):
        for copy in flights[name, q]:
            copy.wait_recv()

    def rows_at(first, size):
        return pl.ds(pl.multiple_of(first, 8), size)

    def stage_compute(q):
        if q == 0:
            load_test.wait()
        loads[q].wait()
        tile = 256

        @pl.loop(0, rc // tile)
        def _(i):
            at = rows_at(q * rc + i * tile, tile)
            part[at, :] = jnp.dot(slab[at, :], test[...], preferred_element_type=F32)

        if q == 0:
            pl.semaphore_wait(barrier, len(peers))
        src = part.at[rows_at(q * rc + (1 - c) * hr, hr)]
        start("core", q, [remote(src, core_in.at[q], core_sem, (q,), core_peer)])

    def stage_core(q):
        arrive("core", q)
        half[q] = part[rows_at(q * rc + c * hr, hr), :] + core_in[q]
        start("x", q, [
            remote(half.at[q, rows_at(p * xr, xr)], x_in.at[q, d], x_sem, (q, d), device(z, p, c))
            for d, p in enumerate(x_peers)
        ])

    def stage_x(q):
        arrive("x", q)
        total = half[q, rows_at(x * xr, xr), :]
        for d in range(nx - 1):
            total = total + x_in[q, d]
        quarter[q] = total
        start("z", q, [
            remote(quarter.at[q, rows_at(p * own, own)], z_in.at[q, d], z_sem, (q, d), device(p, x, c))
            for d, p in enumerate(z_peers)
        ])

    def stage_z(q):
        arrive("z", q)
        total = quarter[q, rows_at(z * own, own), :]
        for d in range(nz - 1):
            total = total + z_in[q, d]
        at = rows_at(q * rc + c * hr + x * xr + z * own, own)
        sketch[at, :] = total
        start("gz", q, [
            remote(sketch.at[at], sketch.at[at], gz_sem, (q, d), device(p, x, c))
            for d, p in enumerate(z_peers)
        ])

    def stage_gz(q):
        arrive("gz", q)
        at = rows_at(q * rc + c * hr + x * xr, xr)
        start("gx", q, [
            remote(sketch.at[at], sketch.at[at], gx_sem, (q, d), device(z, p, c))
            for d, p in enumerate(x_peers)
        ])

    def stage_gx(q):
        arrive("gx", q)
        at = rows_at(q * rc + c * hr, hr)
        start("gc", q, [remote(sketch.at[at], sketch.at[at], gc_sem, (q,), core_peer)])

    def stage_gc(q):
        arrive("gc", q)
        at = pl.ds(q * rc, rc)
        block = sketch[at, :]
        turned = block.T
        gram = jnp.dot(turned, block, precision=HIGHEST, preferred_element_type=F32)
        gram_ref[...] = gram if q == 0 else gram_ref[...] + gram
        high = turned.astype(BF16)
        split[0:k, :] = high
        split[k:2 * k, :] = (turned - high.astype(F32)).astype(BF16)
        tile = 256

        @pl.loop(0, width // tile)
        def _(i):
            cols = pl.ds(pl.multiple_of(i * tile, tile), tile)
            both = jnp.dot(split[...], slab[at, cols], preferred_element_type=F32)
            cross = both[0:k] + both[k:2 * k]
            cross_ref[:, cols] = cross if q == 0 else cross_ref[:, cols] + cross

    stages = [stage_compute, stage_core, stage_x, stage_z, stage_gz, stage_gx, stage_gc]
    begin = [0, 2, 5, 8, 11, 13, 15]
    order = sorted((q + begin[s], -s, q) for s in range(len(stages)) for q in range(nch))
    for _, s, q in order:
        stages[-s](q)
    for copy in sent:
        copy.wait_send()


def factor_kernel(gram_ref, cross_ref, out_ref, work, inverse, split):
    k = gram_ref.shape[0]
    block, panel, lanes = 32, 8, 128
    work[:, 0:k] = gram_ref[...]
    row_at = lax.broadcasted_iota(jnp.int32, (k, k), 0)
    col_at = lax.broadcasted_iota(jnp.int32, (k, k), 1)
    work[:, k:2 * k] = (row_at == col_at).astype(F32)
    sub = lax.broadcasted_iota(jnp.int32, (block, lanes), 0)
    for b in range(k // block):
        first = b * block
        strips = [work[first:first + block, j * lanes:(j + 1) * lanes] for j in range(2 * k // lanes)]
        scale = jnp.zeros((block, lanes), F32)
        for p in range(block // panel):
            base = first + p * panel
            strip, lane = base // lanes, base % lanes
            columns = [
                jnp.broadcast_to(strips[strip][:, lane + i:lane + i + 1], (block, lanes)) for i in range(panel)
            ]
            for i in range(panel):
                r = p * panel + i
                pivot = columns[i][r:r + 1, :]
                scale = jnp.where(sub == r, lax.rsqrt(pivot), scale)
                if r + 1 == block:
                    continue
                lower = jnp.where(sub > r, columns[i] * (1.0 / pivot), 0.0)
                for j in range(i + 1, panel):
                    columns[j] = columns[j] - lower * columns[j][r:r + 1, :]
                strips = [s - lower * s[r:r + 1, :] for s in strips]
        done = jnp.concatenate([s * scale for s in strips], axis=1)
        inverse[first:first + block, :] = done[:, k:2 * k]
        if first + block < k:
            after = first + block
            update = lax.dot_general(
                done[:, after:k], done, (((0,), (0,)), ((), ())),
                precision=HIGHEST, preferred_element_type=F32,
            )
            work[after:k, :] = work[after:k, :] - update

    high = inverse[...].astype(BF16)
    split[0:k, :] = high
    split[k:2 * k, :] = (inverse[...] - high.astype(F32)).astype(BF16)
    tile = 256

    @pl.loop(0, cross_ref.shape[1] // tile)
    def _(i):
        cols = pl.ds(pl.multiple_of(i * tile, tile), tile)
        term = cross_ref[:, cols]
        term_high = term.astype(BF16)
        term_low = (term - term_high.astype(F32)).astype(BF16)
        both = jnp.dot(split[...], term_high, preferred_element_type=F32)
        rest = jnp.dot(split[0:k, :], term_low, preferred_element_type=F32)
        out_ref[:, cols] = both[0:k] + (both[k:2 * k] + rest)


def local(ncol, slab, test):
    rows, width = slab.shape
    k = test.shape[1]
    chips = ncol // 2
    nx = 2 ** (chips.bit_length() // 3) if chips > 1 else 1
    nz = chips // nx
    nch = max(1, min(8, rows // (8 * ncol)))
    rc = rows // nch
    hr, xr, own = rc // 2, rc // (2 * nx), rc // ncol
    dma = pltpu.SemaphoreType.DMA
    gram, cross = pl.pallas_call(
        functools.partial(sketch_kernel, nx, nz, nch),
        out_shape=(jax.ShapeDtypeStruct((k, k), F32), jax.ShapeDtypeStruct((k, width), F32)),
        in_specs=[pl.BlockSpec(memory_space=pl.ANY)] * 2,
        out_specs=(pl.BlockSpec(memory_space=pltpu.VMEM),) * 2,
        scratch_shapes=[
            pltpu.VMEM((rows, width), BF16),
            pltpu.VMEM((width, k), BF16),
            pltpu.VMEM((rows, k), F32),
            pltpu.VMEM((nch, hr, k), F32),
            pltpu.VMEM((nch, hr, k), F32),
            pltpu.VMEM((nch, nx - 1, xr, k), F32),
            pltpu.VMEM((nch, xr, k), F32),
            pltpu.VMEM((nch, nz - 1, own, k), F32),
            pltpu.VMEM((rows, k), F32),
            pltpu.VMEM((2 * k, rc), BF16),
            dma((nch + 1,)),
            dma((2, nch)),
            dma((2, nch, nx - 1)),
            dma((2, nch, nz - 1)),
            dma((2, nch, nz - 1)),
            dma((2, nch, nx - 1)),
            dma((2, nch)),
        ],
        compiler_params=pltpu.CompilerParams(
            collective_id=0, has_side_effects=True, vmem_limit_bytes=48 * 2 ** 20
        ),
    )(slab, test)
    return pl.pallas_call(
        factor_kernel,
        out_shape=jax.ShapeDtypeStruct((k, width), F32),
        in_specs=[pl.BlockSpec(memory_space=pltpu.VMEM)] * 2,
        out_specs=pl.BlockSpec(memory_space=pltpu.VMEM),
        scratch_shapes=[pltpu.VMEM((k, 2 * k), F32), pltpu.VMEM((k, k), F32), pltpu.VMEM((2 * k, k), BF16)],
        compiler_params=pltpu.CompilerParams(vmem_limit_bytes=32 * 2 ** 20),
    )(gram, cross)


def solution(mesh):
    return jax.shard_map(
        functools.partial(local, mesh.shape["col"]),
        mesh=mesh,
        in_specs=(P("groups", "col"), P("col", None)),
        out_specs=P("groups", "col"),
        check_vma=False,
    )
```

```python
import functools

import jax
import jax.numpy as jnp
from jax import lax
from jax.experimental import pallas as pl
from jax.experimental.pallas import tpu as pltpu
from jax.sharding import PartitionSpec as P

F32 = jnp.float32
BF16 = jnp.bfloat16
MESH = pl.DeviceIdType.MESH
HIGHEST = lax.Precision.HIGHEST


def sketch_kernel(
    nx, nz, nch, slab_hbm, test_hbm, gram_ref, cross_ref,
    slab, test, part, core_in, half, x_in, quarter, z_in, sketch, split,
    load_sem, core_sem, x_sem, z_sem, gz_sem, gx_sem, gc_sem,
):
    ncol = 2 * nx * nz
    rows, width = slab.shape
    k = test.shape[1]
    rc = rows // nch
    hr, xr, own = rc // 2, rc // (2 * nx), rc // ncol
    me = lax.axis_index("col")
    c = lax.rem(me, 2)
    x = lax.rem(me // 2, nx)
    z = me // (2 * nx)

    def device(z_, x_, c_):
        return {"col": (z_ * nx + x_) * 2 + c_}

    core_peer = device(z, x, 1 - c)
    x_peers = [lax.rem(x + d, nx) for d in range(1, nx)]
    z_peers = [lax.rem(z + d, nz) for d in range(1, nz)]

    load_test = pltpu.make_async_copy(test_hbm, test, load_sem.at[nch])
    load_test.start()
    loads = []
    for q in range(nch):
        at = pl.ds(q * rc, rc)
        load = pltpu.make_async_copy(slab_hbm.at[at], slab.at[at], load_sem.at[q])
        load.start()
        loads.append(load)

    barrier = pltpu.get_barrier_semaphore()
    peers = [core_peer] + [device(z, p, c) for p in x_peers] + [device(p, x, c) for p in z_peers]
    for peer in peers:
        pl.semaphore_signal(barrier, inc=1, device_id=peer, device_id_type=MESH)

    def remote(src, dst, sems, index, peer):
        return pltpu.make_async_remote_copy(
            src_ref=src, dst_ref=dst,
            send_sem=sems.at[(0,) + index], recv_sem=sems.at[(1,) + index],
            device_id=peer, device_id_type=MESH,
        )

    sent = []
    flights = {}

    def start(name, q, copies):
        for copy in copies:
            copy.start()
        sent.extend(copies)
        flights[name, q] = copies

    def arrive(name, q):
        for copy in flights[name, q]:
            copy.wait_recv()

    def rows_at(first, size):
        return pl.ds(pl.multiple_of(first, 8), size)

    def stage_compute(q):
        if q == 0:
            load_test.wait()
        loads[q].wait()
        tile = 256

        @pl.loop(0, rc // tile)
        def _(i):
            at = rows_at(q * rc + i * tile, tile)
            part[at, :] = jnp.dot(slab[at, :], test[...], preferred_element_type=F32)

        if q == 0:
            pl.semaphore_wait(barrier, len(peers))
        src = part.at[rows_at(q * rc + (1 - c) * hr, hr)]
        start("core", q, [remote(src, core_in.at[q], core_sem, (q,), core_peer)])

    def stage_core(q):
        arrive("core", q)
        half[q] = part[rows_at(q * rc + c * hr, hr), :] + core_in[q]
        start("x", q, [
            remote(half.at[q, rows_at(p * xr, xr)], x_in.at[q, d], x_sem, (q, d), device(z, p, c))
            for d, p in enumerate(x_peers)
        ])

    def stage_x(q):
        arrive("x", q)
        total = half[q, rows_at(x * xr, xr), :]
        for d in range(nx - 1):
            total = total + x_in[q, d]
        quarter[q] = total
        start("z", q, [
            remote(quarter.at[q, rows_at(p * own, own)], z_in.at[q, d], z_sem, (q, d), device(p, x, c))
            for d, p in enumerate(z_peers)
        ])

    def stage_z(q):
        arrive("z", q)
        total = quarter[q, rows_at(z * own, own), :]
        for d in range(nz - 1):
            total = total + z_in[q, d]
        at = rows_at(q * rc + c * hr + x * xr + z * own, own)
        sketch[at, :] = total
        start("gz", q, [
            remote(sketch.at[at], sketch.at[at], gz_sem, (q, d), device(p, x, c))
            for d, p in enumerate(z_peers)
        ])

    def stage_gz(q):
        arrive("gz", q)
        at = rows_at(q * rc + c * hr + x * xr, xr)
        start("gx", q, [
            remote(sketch.at[at], sketch.at[at], gx_sem, (q, d), device(z, p, c))
            for d, p in enumerate(x_peers)
        ])

    def stage_gx(q):
        arrive("gx", q)
        at = rows_at(q * rc + c * hr, hr)
        start("gc", q, [remote(sketch.at[at], sketch.at[at], gc_sem, (q,), core_peer)])

    def stage_gc(q):
        arrive("gc", q)
        at = pl.ds(q * rc, rc)
        block = sketch[at, :]
        turned = block.T
        gram = jnp.dot(turned, block, precision=HIGHEST, preferred_element_type=F32)
        gram_ref[...] = gram if q == 0 else gram_ref[...] + gram
        high = turned.astype(BF16)
        split[0:k, :] = high
        split[k:2 * k, :] = (turned - high.astype(F32)).astype(BF16)
        tile = 256

        @pl.loop(0, width // tile)
        def _(i):
            cols = pl.ds(pl.multiple_of(i * tile, tile), tile)
            both = jnp.dot(split[...], slab[at, cols], preferred_element_type=F32)
            cross = both[0:k] + both[k:2 * k]
            cross_ref[:, cols] = cross if q == 0 else cross_ref[:, cols] + cross

    stages = [stage_compute, stage_core, stage_x, stage_z, stage_gz, stage_gx, stage_gc]
    begin = [0, 2, 5, 8, 11, 13, 15]
    order = sorted((q + begin[s], -s, q) for s in range(len(stages)) for q in range(nch))
    for _, s, q in order:
        stages[-s](q)
    for copy in sent:
        copy.wait_send()


def factor_kernel(gram_ref, cross_ref, out_ref, work, inverse, split):
    k = gram_ref.shape[0]
    block, panel, lanes = 32, 8, 128
    work[:, 0:k] = gram_ref[...]
    row_at = lax.broadcasted_iota(jnp.int32, (k, k), 0)
    col_at = lax.broadcasted_iota(jnp.int32, (k, k), 1)
    work[:, k:2 * k] = (row_at == col_at).astype(F32)
    sub = lax.broadcasted_iota(jnp.int32, (block, lanes), 0)
    for b in range(k // block):
        first = b * block
        low = first // lanes
        left, right = low * lanes, k + (low + 1) * lanes
        strips = [work[first:first + block, j:j + lanes] for j in range(left, right, lanes)]
        scale = jnp.zeros((block, lanes), F32)
        for p in range(block // panel):
            base = first + p * panel
            strip, lane = base // lanes - low, base % lanes
            columns = [
                jnp.broadcast_to(strips[strip][:, lane + i:lane + i + 1], (block, lanes)) for i in range(panel)
            ]
            for i in range(panel):
                r = p * panel + i
                pivot = columns[i][r:r + 1, :]
                scale = jnp.where(sub == r, lax.rsqrt(pivot), scale)
                if r + 1 == block:
                    continue
                lower = jnp.where(sub > r, columns[i] * (1.0 / pivot), 0.0)
                for j in range(i + 1, panel):
                    columns[j] = columns[j] - lower * columns[j][r:r + 1, :]
                strips = [s - lower * s[r:r + 1, :] for s in strips]
        done = jnp.concatenate([s * scale for s in strips], axis=1)
        inverse[first:first + block, 0:right - k] = done[:, k - left:]
        if right < 2 * k:
            inverse[first:first + block, right - k:] = jnp.zeros((block, 2 * k - right), F32)
        if first + block < k:
            after = first + block
            update = lax.dot_general(
                done[:, after - left:k - left], done, (((0,), (0,)), ((), ())),
                precision=HIGHEST, preferred_element_type=F32,
            )
            work[after:k, left:right] = work[after:k, left:right] - update

    high = inverse[...].astype(BF16)
    split[0:k, :] = high
    split[k:2 * k, :] = (inverse[...] - high.astype(F32)).astype(BF16)
    tile = 256

    @pl.loop(0, cross_ref.shape[1] // tile)
    def _(i):
        cols = pl.ds(pl.multiple_of(i * tile, tile), tile)
        term = cross_ref[:, cols]
        term_high = term.astype(BF16)
        term_low = (term - term_high.astype(F32)).astype(BF16)
        both = jnp.dot(split[...], term_high, preferred_element_type=F32)
        rest = jnp.dot(split[0:k, :], term_low, preferred_element_type=F32)
        out_ref[:, cols] = both[0:k] + (both[k:2 * k] + rest)


def local(ncol, slab, test):
    rows, width = slab.shape
    k = test.shape[1]
    chips = ncol // 2
    nx = 2 ** (chips.bit_length() // 3) if chips > 1 else 1
    nz = chips // nx
    nch = max(1, min(8, rows // (8 * ncol)))
    rc = rows // nch
    hr, xr, own = rc // 2, rc // (2 * nx), rc // ncol
    dma = pltpu.SemaphoreType.DMA
    gram, cross = pl.pallas_call(
        functools.partial(sketch_kernel, nx, nz, nch),
        out_shape=(jax.ShapeDtypeStruct((k, k), F32), jax.ShapeDtypeStruct((k, width), F32)),
        in_specs=[pl.BlockSpec(memory_space=pl.ANY)] * 2,
        out_specs=(pl.BlockSpec(memory_space=pltpu.VMEM),) * 2,
        scratch_shapes=[
            pltpu.VMEM((rows, width), BF16),
            pltpu.VMEM((width, k), BF16),
            pltpu.VMEM((rows, k), F32),
            pltpu.VMEM((nch, hr, k), F32),
            pltpu.VMEM((nch, hr, k), F32),
            pltpu.VMEM((nch, nx - 1, xr, k), F32),
            pltpu.VMEM((nch, xr, k), F32),
            pltpu.VMEM((nch, nz - 1, own, k), F32),
            pltpu.VMEM((rows, k), F32),
            pltpu.VMEM((2 * k, rc), BF16),
            dma((nch + 1,)),
            dma((2, nch)),
            dma((2, nch, nx - 1)),
            dma((2, nch, nz - 1)),
            dma((2, nch, nz - 1)),
            dma((2, nch, nx - 1)),
            dma((2, nch)),
        ],
        compiler_params=pltpu.CompilerParams(
            collective_id=0, has_side_effects=True, vmem_limit_bytes=48 * 2 ** 20
        ),
    )(slab, test)
    return pl.pallas_call(
        factor_kernel,
        out_shape=jax.ShapeDtypeStruct((k, width), F32),
        in_specs=[pl.BlockSpec(memory_space=pltpu.VMEM)] * 2,
        out_specs=pl.BlockSpec(memory_space=pltpu.VMEM),
        scratch_shapes=[pltpu.VMEM((k, 2 * k), F32), pltpu.VMEM((k, k), F32), pltpu.VMEM((2 * k, k), BF16)],
        compiler_params=pltpu.CompilerParams(vmem_limit_bytes=32 * 2 ** 20),
    )(gram, cross)


def solution(mesh):
    return jax.shard_map(
        functools.partial(local, mesh.shape["col"]),
        mesh=mesh,
        in_specs=(P("groups", "col"), P("col", None)),
        out_specs=P("groups", "col"),
        check_vma=False,
    )
```
